256 devices in a mesh: pipe: 8 (over x, y_hi), ep: 32 (over z, y_lo, core).
Axes of the slice: x: 4, y: 4 (y_hi: 2, y_lo: 2; y = y_hi * 2 + y_lo), z: 8, core: 2. Of those that a mesh axis runs over, the one named last changes fastest.
Arguments:
- acts: bfloat16 [32768, 3584], P(('pipe', 'ep')), may hold values from -6 to 6
- cotan: bfloat16 [32768, 3584], P(('pipe', 'ep')), may hold values from -6 to 6
- routes: int32 [32768, 8], P(('pipe', 'ep')), may hold values from 0 to 255, all different within a row; in each aligned block of 128 rows (0 to 127, 128 to 255, ...) at most 8 rows name the same one
- scores: float32 [32768, 8], P(('pipe', 'ep')), may hold values from 0.05 to 1
- w_gate: bfloat16 [8, 3584, 12288], P('pipe', None, 'ep'), may hold values from -0.09375 to 0.09375
- w_up: bfloat16 [8, 3584, 12288], P('pipe', None, 'ep'), may hold values from -0.09375 to 0.09375
- w_down: bfloat16 [8, 12288, 3584], P('pipe', 'ep'), may hold values from -0.15625 to 0.15625
Outputs:
- next_acts: bfloat16 [32768, 3584], P(('pipe', 'ep'))
- prev_grads: bfloat16 [32768, 3584], P(('pipe', 'ep'))
The draws below stay inside these ranges and needn't reach their ends.
Inputs may be any that keep to these rules, and one draw needn't show every extreme that they name: `routes`: in the rows of one device no expert is named by more than 8 rows; a row names 8 different experts.
All inputs are finite; a program needn't handle non-finite values.
Results may differ from the reference program's by a relative error of at most 0.015.
Values may be sent and summed in bfloat16 or wider, within the bound.
No kernel may reach another device: no remote copies, remote signals or barrier semaphores. Data moves between devices by JAX's collectives and lax.ppermute only.
A program may use at most 64 MiB of HBM per device.

```python
import math
import jax
import jax.numpy as jnp
import numpy as np
from jax import lax

D = 3584
EXPERTS = 256
TOPK = 8
FF = 1536
SHARDS = 4
TOK_DEV = 128
CAP = 8
FF_DEV = 384
E_FLY = 8
HIDDEN_ALL = 12288
ALL_TOK = 32768
N_PIPE = 8
N_EP = 32


def block_levels(stream_key, dims, cuts, smallest, largest):
    factor_of = 1.0
    for dim, blocks in cuts:
        heights = jax.random.uniform(jax.random.fold_in(jax.random.fold_in(stream_key, 6), dim), (blocks,), jnp.float32, smallest / len(cuts), largest / len(cuts))
        factor_of = factor_of * jnp.repeat(jnp.exp(heights), dims[dim] // blocks).reshape((-1,) + (1,) * (len(dims) - 1 - dim))
    return factor_of


def deal_out(stream_key, own, number, rows, number_of, top, most, slope):
    ranking = jax.random.permutation(stream_key, number_of)
    packed, usual = shares(number_of, rows * top, most, slope, True), shares(number_of, rows * top, most, slope, False)
    places = jnp.arange(number_of)

    def named(tallies, rotation):
        used = int((tallies > 0).sum())
        fixed = max(1, used // 4)
        shifted = fixed + (places - fixed + rotation * (used - fixed)) % max(1, number_of - fixed)
        return jnp.zeros((number_of,), jnp.int32).at[ranking[jnp.where(places < fixed, places, shifted)]].set(jnp.asarray(tallies, jnp.int32))

    tallies = jnp.where(number % 4 == 0, named(packed, number // 4), named(usual, number - number // 4 - 1))
    mixed = jax.random.permutation(jax.random.fold_in(own, 3), number_of)
    source_of, taker = mixed[0:number_of // 2 * 2:2], mixed[1:number_of // 2 * 2:2]
    margin = jnp.minimum(tallies[source_of] - 1, most - tallies[taker]) // 2
    margin = jnp.where((source_of == ranking[0]) | (taker == ranking[0]) | (tallies[taker] == 0), 0, jnp.maximum(margin, 0))
    shifted = jax.random.randint(jax.random.fold_in(own, 4), (number_of // 2,), 0, 1 << 20) % (margin + 1)
    tallies = tallies.at[source_of].add(-shifted).at[taker].add(shifted)
    members = jnp.searchsorted(jnp.cumsum(tallies), jnp.arange(rows * top), side="right").astype(jnp.int32)
    table = members.reshape(top, rows).T
    table = table[jax.random.permutation(jax.random.fold_in(own, 1), rows)]
    rotation = jax.random.randint(jax.random.fold_in(own, 2), (rows, 1), 0, top)
    return jnp.take_along_axis(table, (jnp.arange(top)[None, :] + rotation) % top, axis=1)


def shares(count, total, most, lean, full):
    portions = [(1 << 20) // math.isqrt(rank ** lean) + 1 for rank in range(1, count + 1)]
    largest = most if full else min(most, max(-(-total // count), total * portions[0] // sum(portions)))
    least = 1 if total - largest >= count - 1 else 0
    holding, surplus = [largest] + [least] * (count - 1), total - largest - least * (count - 1)
    while surplus > 0:
        candidates = [i for i in range(1, count) if holding[i] < largest] or [i for i in range(1, count) if holding[i] < most]
        pool, left = sum([portions[i] for i in candidates]), surplus
        for i in candidates:
            extra = min(most - holding[i], max(1, left * portions[i] // pool), surplus)
            holding[i] = holding[i] + extra
            surplus = surplus - extra
    return np.array(holding)


def noise(stream_key, shape, width, most, cuts=(), kind=jnp.bfloat16):
    array = jax.random.normal(stream_key, shape, jnp.float32) * width
    if len(cuts) > 0:
        array = block_levels(stream_key, shape, cuts, -0.22, 0.18) * array
    return jnp.clip(array, min=-most, max=most).astype(kind)


def setup_inputs(seed: int = 0) -> dict:
    splits = jax.random.split(jax.random.key(seed), 8)
    acts = noise(splits[0], (ALL_TOK, D), 1.0, 6.0, ((0, 256),))
    cotan = noise(splits[1], (ALL_TOK, D), 1.0, 6.0, ((0, 256),))
    routes_keys = jax.random.split(jax.random.fold_in(splits[2], 1), ALL_TOK // TOK_DEV)
    routes_turns = jax.random.permutation(jax.random.fold_in(splits[2], 3), ALL_TOK // TOK_DEV)
    routes = jax.vmap(lambda own, number: deal_out(jax.random.fold_in(splits[2], 2), own, number, TOK_DEV, EXPERTS, TOPK, CAP, 2))(routes_keys, routes_turns).reshape((ALL_TOK, TOPK))
    scores = jnp.clip(jnp.exp(math.log(1.0) - 2.9957323 * jax.random.uniform(splits[3], (ALL_TOK, TOPK), jnp.float32) ** block_levels(splits[3], (ALL_TOK, TOPK), ((0, 256),), -0.2, 0.2)), 0.05, 1.0)
    w_gate = noise(splits[4], (N_PIPE, D, HIDDEN_ALL), D ** -0.5, 0.09375, ((0, 8), (2, 32)))
    w_up = noise(splits[5], (N_PIPE, D, HIDDEN_ALL), D ** -0.5, 0.09375, ((0, 8), (2, 32)))
    w_down = noise(splits[6], (N_PIPE, HIDDEN_ALL, D), FF ** -0.5, 0.15625, ((0, 8), (1, 32)))
    return dict(acts=acts, cotan=cotan, routes=routes, scores=scores, w_gate=w_gate, w_up=w_up, w_down=w_down)


ROUTE_SCALE = 2.5


def one_section(inputs):
    tokens, grads, route_ids, route_scores, gate_mat, up_mat, down_mat = inputs
    norm_w = route_scores / jnp.sum(route_scores, axis=-1, keepdims=True) * ROUTE_SCALE
    match = route_ids[..., None] == jnp.arange(E_FLY, dtype=jnp.int32)
    member = jnp.sum(match.astype(jnp.int32), axis=2)
    weight_te = jnp.sum(jnp.where(match, norm_w[..., None], jnp.zeros_like(norm_w[..., None])), axis=2)
    slot_of = jnp.cumsum(member, axis=1) - member
    placed = ((member[..., None] == 1) & (slot_of[..., None] == jnp.arange(CAP, dtype=jnp.int32))).astype(jnp.float32)
    buf_x = jnp.einsum('btec,btd->ebcd', placed, tokens.astype(jnp.float32)).astype(jnp.bfloat16)
    buf_g = jnp.einsum('btec,btd->ebcd', placed, grads.astype(jnp.float32)).astype(jnp.bfloat16)
    row_block = buf_x.reshape(E_FLY, N_EP * CAP, D).astype(jnp.float32)
    grad_block = buf_g.reshape(E_FLY, N_EP * CAP, D).astype(jnp.float32)
    gate_w = gate_mat.astype(jnp.float32).reshape(D, E_FLY, SHARDS, FF_DEV)
    up_w = up_mat.astype(jnp.float32).reshape(D, E_FLY, SHARDS, FF_DEV)
    down_w = down_mat.astype(jnp.float32).reshape(E_FLY, SHARDS, FF_DEV, D)
    gate_val = jnp.einsum('erd,dekf->ekrf', row_block, gate_w)
    up_val = jnp.einsum('erd,dekf->ekrf', row_block, up_w)
    sig_val = jax.nn.sigmoid(gate_val)
    hidden = (gate_val * sig_val * up_val).astype(jnp.bfloat16)
    parts = jnp.einsum('ekrf,ekfd->ekrd', hidden.astype(jnp.float32), down_w).astype(jnp.bfloat16)
    expert_out = jnp.sum(parts.astype(jnp.float32), axis=1)
    d_hidden = jnp.einsum('erd,ekfd->ekrf', grad_block, down_w)
    d_gate = (d_hidden * up_val * sig_val * (1.0 + gate_val * (1.0 - sig_val))).astype(jnp.bfloat16)
    d_up = (d_hidden * gate_val * sig_val).astype(jnp.bfloat16)
    grad_parts = (jnp.einsum('ekrf,dekf->ekrd', d_gate.astype(jnp.float32), gate_w)
                  + jnp.einsum('ekrf,dekf->ekrd', d_up.astype(jnp.float32), up_w)).astype(jnp.bfloat16)
    grad_sum = jnp.sum(grad_parts.astype(jnp.float32), axis=1)
    mixing = placed * weight_te[..., None]
    result = jnp.einsum('btec,ebcd->btd', mixing, expert_out.reshape(E_FLY, N_EP, CAP, D),
                        precision=lax.Precision.HIGHEST).astype(jnp.bfloat16)
    grad_result = jnp.einsum('btec,ebcd->btd', mixing, grad_sum.reshape(E_FLY, N_EP, CAP, D),
                             precision=lax.Precision.HIGHEST).astype(jnp.bfloat16)
    return result, grad_result


def reference(acts, cotan, routes, scores, w_gate, w_up, w_down):
    grid = (N_PIPE, N_EP, TOK_DEV, D)
    small = (N_PIPE, N_EP, TOK_DEV, TOPK)
    stacked = (acts.reshape(grid), cotan.reshape(grid), routes.reshape(small), scores.reshape(small),
               w_gate, w_up, w_down)
    outputs, input_grads = lax.map(one_section, stacked)
    next_acts = jnp.roll(outputs, 1, axis=0).reshape(N_PIPE * N_EP * TOK_DEV, D)
    prev_grads = jnp.roll(input_grads, -1, axis=0).reshape(N_PIPE * N_EP * TOK_DEV, D)
    return next_acts, prev_grads
```

```python
import jax
import jax.numpy as jnp
from jax import lax
from jax.sharding import PartitionSpec as P

ROUTE_SCALE = 2.5
N_X, N_YH, N_Z, N_Y, N_C = 4, 2, 8, 2, 2
N_EP = N_Z * N_Y * N_C
AXES = ("pipe", "ep")
SLOTS = 8


def permutation(target):
    pairs = []
    for s in range(N_X * N_YH):
        for i in range(N_EP):
            z, y, c = i // 4, (i // 2) % 2, i % 2
            s2, z2, y2, c2 = target(s, z, y, c)
            pairs.append((s * N_EP + i, (s2 % 8) * N_EP + (z2 % N_Z) * 4 + y2 * 2 + c2))
    return pairs


TO_Y = permutation(lambda s, z, y, c: (s, z, 1 - y, c))
TO_CORE = permutation(lambda s, z, y, c: (s, z, y, 1 - c))
NEXT_FLIP = permutation(lambda s, z, y, c: (s + 1, z, 1 - y, c))
PREV_FLIP = permutation(lambda s, z, y, c: (s - 1, z, 1 - y, c))
NEXT = permutation(lambda s, z, y, c: (s + 1, z, y, c))
PREV = permutation(lambda s, z, y, c: (s - 1, z, y, c))
Z_GROUPS = [[z * 4 + q for z in range(N_Z)] for q in range(4)]


def over_z(values):
    return lax.all_to_all(values, "ep", 0, 0, axis_index_groups=Z_GROUPS, tiled=True)


def gather_quad(own):
    both = jnp.concatenate([own, lax.ppermute(own, AXES, TO_Y)], axis=0)
    return jnp.concatenate([both, lax.ppermute(both, AXES, TO_CORE)], axis=0)


def scatter_quad(parts, flip):
    width = parts.shape[-1]
    half = parts.shape[0] // 2
    got = lax.ppermute(parts[half:].astype(jnp.bfloat16), AXES, TO_CORE)
    chip = parts[:half] + got.astype(jnp.float32)
    quarter = half // 2
    got = lax.ppermute(chip[:quarter].astype(jnp.bfloat16), AXES, TO_Y)
    done = (chip[quarter:] + got.astype(jnp.float32)).astype(jnp.bfloat16)
    moved = lax.ppermute(done, AXES, flip)
    return over_z(moved.reshape(N_Z, SLOTS, width)).reshape(N_Z * SLOTS, width)


def mix(combine, values):
    hi = combine.astype(jnp.bfloat16)
    rest = combine - hi.astype(jnp.float32)
    mid = rest.astype(jnp.bfloat16)
    low = (rest - mid.astype(jnp.float32)).astype(jnp.bfloat16)
    lhs = jnp.concatenate([hi, mid, low], axis=1)
    rhs = jnp.concatenate([values, values, values], axis=0)
    return jnp.dot(lhs, rhs, preferred_element_type=jnp.float32).astype(jnp.bfloat16)


def shards(acts, cotan, routes, scores, w_gate, w_up, w_down):
    tok_rows, width = acts.shape
    gate_mat, up_mat, down_mat = w_gate[0], w_up[0], w_down[0]
    norm_w = scores / jnp.sum(scores, axis=1, keepdims=True) * ROUTE_SCALE
    match = routes[:, :, None] == jnp.arange(N_Z, dtype=jnp.int32)
    member = jnp.sum(match.astype(jnp.int32), axis=1)
    weight_te = jnp.sum(jnp.where(match, norm_w[:, :, None], 0.0), axis=1)
    slot_of = jnp.cumsum(member, axis=0) - member
    placed = (member[:, :, None] == 1) & (slot_of[:, :, None] == jnp.arange(SLOTS, dtype=jnp.int32))
    dispatch = placed.reshape(tok_rows, N_Z * SLOTS).T.astype(jnp.bfloat16)
    combine = (placed.astype(jnp.float32) * weight_te[:, :, None]).reshape(tok_rows, N_Z * SLOTS)

    def pack(values):
        rows = jnp.dot(dispatch, values, preferred_element_type=jnp.float32).astype(jnp.bfloat16)
        return rows.reshape(N_Z, SLOTS, width)

    x_own = over_z(pack(acts)).reshape(N_Z * SLOTS, width)
    g_own = over_z(pack(cotan)).reshape(N_Z * SLOTS, width)
    combine_next = lax.ppermute(combine, AXES, NEXT)
    combine_prev = lax.ppermute(combine, AXES, PREV)
    x = gather_quad(x_own)
    gate_val = jnp.dot(x, gate_mat, preferred_element_type=jnp.float32)
    up_val = jnp.dot(x, up_mat, preferred_element_type=jnp.float32)
    sig_val = jax.nn.sigmoid(gate_val)
    hidden = (gate_val * sig_val * up_val).astype(jnp.bfloat16)
    expert_out = jnp.dot(hidden, down_mat, preferred_element_type=jnp.float32)
    out_rows = scatter_quad(expert_out, NEXT_FLIP)
    g = gather_quad(g_own)
    contract = (((1,), (1,)), ((), ()))
    d_hidden = lax.dot_general(g, down_mat, contract, preferred_element_type=jnp.float32)
    d_gate = (d_hidden * up_val * sig_val * (1.0 + gate_val * (1.0 - sig_val))).astype(jnp.bfloat16)
    d_up = (d_hidden * gate_val * sig_val).astype(jnp.bfloat16)
    grad_in = lax.dot_general(d_gate, gate_mat, contract, preferred_element_type=jnp.float32)
    grad_in = grad_in + lax.dot_general(d_up, up_mat, contract, preferred_element_type=jnp.float32)
    grad_rows = scatter_quad(grad_in, PREV_FLIP)
    return mix(combine_next, out_rows), mix(combine_prev, grad_rows)


def solution(mesh):
    rows = P(AXES, None)
    in_specs = (rows, rows, rows, rows, P("pipe", None, "ep"), P("pipe", None, "ep"), P("pipe", "ep", None))
    return jax.shard_map(shards, mesh=mesh, in_specs=in_specs, out_specs=(rows, rows), check_vma=False)
```

```python
import jax
import jax.numpy as jnp
from jax import lax
from jax.experimental import pallas as pl
from jax.experimental.pallas import tpu as pltpu
from jax.sharding import PartitionSpec as P

ROUTE_SCALE = 2.5
N_X, N_YH, N_Z, N_Y, N_C = 4, 2, 8, 2, 2
N_EP = N_Z * N_Y * N_C
AXES = ("pipe", "ep")
SLOTS = 8
ROWS = N_Z * SLOTS


def permutation(target):
    pairs = []
    for s in range(N_X * N_YH):
        for i in range(N_EP):
            z, y, c = i // 4, (i // 2) % 2, i % 2
            s2, z2, y2, c2 = target(s, z, y, c)
            pairs.append((s * N_EP + i, (s2 % 8) * N_EP + (z2 % N_Z) * 4 + y2 * 2 + c2))
    return pairs


TO_Y = permutation(lambda s, z, y, c: (s, z, 1 - y, c))
TO_CORE = permutation(lambda s, z, y, c: (s, z, y, 1 - c))
NEXT_FLIP = permutation(lambda s, z, y, c: (s + 1, z, 1 - y, c))
PREV_FLIP = permutation(lambda s, z, y, c: (s - 1, z, 1 - y, c))
NEXT = permutation(lambda s, z, y, c: (s + 1, z, y, c))
PREV = permutation(lambda s, z, y, c: (s - 1, z, y, c))
Z_GROUPS = [[z * 4 + q for z in range(N_Z)] for q in range(4)]
K_STEPS = 4
N_STEPS = 7


def over_z(values):
    return lax.all_to_all(values, "ep", 0, 0, axis_index_groups=Z_GROUPS, tiled=True)


def dot(a, b):
    return jnp.dot(a, b, preferred_element_type=jnp.float32)


def dot_t(a, b):
    return lax.dot_general(a, b, (((1,), (1,)), ((), ())), preferred_element_type=jnp.float32)


def fill(rows_scr, pieces):
    at = 0
    for piece in pieces:
        rows_scr[pl.ds(at, piece.shape[0]), :] = piece[...]
        at += piece.shape[0]


def emit_columns(tile, send_ref, keep_ref):
    half, width = keep_ref.shape
    step = width // N_STEPS
    for n in range(N_STEPS):
        cols = pl.ds(n * step, step)
        value = tile(cols)
        keep_ref[:, cols] = value[:half]
        send_ref[:, cols] = value[half:].astype(jnp.bfloat16)


def over_width(rows_scr, mat, product):
    step = rows_scr.shape[1] // K_STEPS
    total = None
    for k in range(K_STEPS):
        part = pl.ds(k * step, step)
        add = product(rows_scr[:, part], mat(part))
        total = add if total is None else total + add
    return total


def forward_kernel(own_ref, y_ref, c_ref, gate_ref, up_ref, down_ref, send_ref, keep_ref, slope_ref, gated_ref, x_scr):
    fill(x_scr, (own_ref, y_ref, c_ref))
    gate_val = over_width(x_scr, lambda part: gate_ref[part, :], dot)
    up_val = over_width(x_scr, lambda part: up_ref[part, :], dot)
    sig_val = jax.nn.sigmoid(gate_val)
    gated = gate_val * sig_val
    gated_ref[...] = gated
    slope_ref[...] = up_val * sig_val * (1.0 + gate_val * (1.0 - sig_val))
    hidden = (gated * up_val).astype(jnp.bfloat16)
    emit_columns(lambda cols: dot(hidden, down_ref[:, cols]), send_ref, keep_ref)


def backward_kernel(own_ref, y_ref, c_ref, gate_ref, up_ref, down_ref, slope_ref, gated_ref, send_ref, keep_ref, g_scr):
    fill(g_scr, (own_ref, y_ref, c_ref))
    d_hidden = over_width(g_scr, lambda part: down_ref[:, part], dot_t)
    d_gate = (d_hidden * slope_ref[...]).astype(jnp.bfloat16)
    d_up = (d_hidden * gated_ref[...]).astype(jnp.bfloat16)
    emit_columns(lambda cols: dot_t(d_gate, gate_ref[cols, :]) + dot_t(d_up, up_ref[cols, :]), send_ref, keep_ref)


VMEM = pl.BlockSpec(memory_space=pltpu.VMEM)


def expert_call(kernel, pieces, gate_mat, up_mat, down_mat, saved, cost):
    width, hid = gate_mat.shape
    rows = sum(p.shape[0] for p in pieces)
    half = rows // 2
    out_shape = [jax.ShapeDtypeStruct((half, width), jnp.bfloat16), jax.ShapeDtypeStruct((half, width), jnp.float32)]
    if not saved:
        out_shape += [jax.ShapeDtypeStruct((rows, hid), jnp.float32)] * 2
    operands = (*pieces, *((m) for m in (gate_mat, up_mat, down_mat)), *saved)
    return pl.pallas_call(
        kernel,
        out_shape=out_shape,
        in_specs=[VMEM] * len(operands),
        out_specs=[VMEM] * len(out_shape),
        scratch_shapes=[pltpu.VMEM((rows, width), jnp.bfloat16)],
        compiler_params=pltpu.CompilerParams(vmem_limit_bytes=40 * 2**20),
        cost_estimate=pl.CostEstimate(flops=cost, bytes_accessed=12_000_000, transcendentals=0),
    )(*operands)


def mix(combine, values):
    hi = combine.astype(jnp.bfloat16)
    rest = combine - hi.astype(jnp.float32)
    mid = rest.astype(jnp.bfloat16)
    low = (rest - mid.astype(jnp.float32)).astype(jnp.bfloat16)
    lhs = jnp.concatenate([hi, mid, low], axis=1)
    rhs = jnp.concatenate([values, values, values], axis=0)
    return dot(lhs, rhs).astype(jnp.bfloat16)


def shards(acts, cotan, routes, scores, w_gate, w_up, w_down):
    tok_rows, width = acts.shape
    gate_mat, up_mat, down_mat = w_gate[0], w_up[0], w_down[0]
    norm_w = scores / jnp.sum(scores, axis=1, keepdims=True) * ROUTE_SCALE
    match = routes[:, :, None] == jnp.arange(N_Z, dtype=jnp.int32)
    member = jnp.sum(match.astype(jnp.int32), axis=1)
    weight_te = jnp.sum(jnp.where(match, norm_w[:, :, None], 0.0), axis=1)
    slot_of = jnp.cumsum(member, axis=0) - member
    placed = (member[:, :, None] == 1) & (slot_of[:, :, None] == jnp.arange(SLOTS, dtype=jnp.int32))
    dispatch = placed.reshape(tok_rows, ROWS).T.astype(jnp.bfloat16)
    combine = (placed.astype(jnp.float32) * weight_te[:, :, None]).reshape(tok_rows, ROWS)

    together = lax.optimization_barrier

    def to(values, table):
        return lax.ppermute(values, AXES, table)

    def back(values):
        return over_z(values.reshape(N_Z, SLOTS, width)).reshape(ROWS, width)

    def halves(keep, got):
        a = (keep[:ROWS] + got[:ROWS].astype(jnp.float32)).astype(jnp.bfloat16)
        return a, keep[ROWS:] + got[ROWS:].astype(jnp.float32)

    def finish(kept, got):
        return (kept + got.astype(jnp.float32)).astype(jnp.bfloat16)

    empty = jnp.zeros_like(placed)
    first = jnp.concatenate([placed, empty], axis=2).reshape(tok_rows, 2 * ROWS).T.astype(jnp.bfloat16)
    second = jnp.concatenate([empty, placed], axis=2).reshape(tok_rows, 2 * ROWS).T.astype(jnp.bfloat16)
    pair = (dot(first, acts) + dot(second, cotan)).astype(jnp.bfloat16)
    pair = over_z(pair.reshape(N_Z, 2 * SLOTS, width))
    x_own, g_own = pair[:, :SLOTS].reshape(ROWS, width), pair[:, SLOTS:].reshape(ROWS, width)
    combine_next = to(combine, NEXT)
    combine_prev = to(combine, PREV)
    x_own, g_own, combine_next, combine_prev = together((x_own, g_own, combine_next, combine_prev))
    x_y = to(x_own, TO_Y)
    x_y, x_own, g_own = together((x_y, x_own, g_own))
    x_c = to(jnp.concatenate([x_own, x_y], axis=0), TO_CORE)
    send, keep, slope, gated = expert_call(forward_kernel, (x_own, x_y, x_c), gate_mat, up_mat, down_mat, (), 20_000_000_000)
    g_y = to(g_own, TO_Y)
    send, keep, slope, gated, g_own, g_y = together((send, keep, slope, gated, g_own, g_y))
    got = to(send, TO_CORE)
    g_c = to(jnp.concatenate([g_own, g_y], axis=0), TO_CORE)
    out_a, out_b = halves(keep, got)
    out_a, out_b, g_c = together((out_a, out_b, g_c))
    out_y = to(out_a, TO_Y)
    send, keep = expert_call(backward_kernel, (g_own, g_y, g_c), gate_mat, up_mat, down_mat, (slope, gated), 20_000_000_000)
    grad_a, grad_b = halves(keep, to(send, TO_CORE))
    out_rows = back(finish(out_b, out_y))
    grad_rows = to(finish(grad_b, to(grad_a, TO_Y)), PREV_FLIP)
    out_rows, grad_rows = together((out_rows, grad_rows))
    out_rows = to(out_rows, NEXT_FLIP)
    grad_rows = back(grad_rows)
    return mix(combine_next, out_rows), mix(combine_prev, grad_rows)


def solution(mesh):
    rows = P(AXES, None)
    in_specs = (rows, rows, rows, rows, P("pipe", None, "ep"), P("pipe", None, "ep"), P("pipe", "ep", None))
    return jax.shard_map(shards, mesh=mesh, in_specs=in_specs, out_specs=(rows, rows), check_vma=False)
```

```python
import jax
import jax.numpy as jnp
from jax import lax
from jax.experimental import pallas as pl
from jax.experimental.pallas import tpu as pltpu
from jax.sharding import PartitionSpec as P

ROUTE_SCALE = 2.5
N_X, N_YH, N_Z, N_Y, N_C = 4, 2, 8, 2, 2
N_EP = N_Z * N_Y * N_C
AXES = ("pipe", "ep")
SLOTS = 8
ROWS = N_Z * SLOTS


def permutation(target):
    pairs = []
    for s in range(N_X * N_YH):
        for i in range(N_EP):
            z, y, c = i // 4, (i // 2) % 2, i % 2
            s2, z2, y2, c2 = target(s, z, y, c)
            pairs.append((s * N_EP + i, (s2 % 8) * N_EP + (z2 % N_Z) * 4 + y2 * 2 + c2))
    return pairs


TO_Y = permutation(lambda s, z, y, c: (s, z, 1 - y, c))
TO_CORE = permutation(lambda s, z, y, c: (s, z, y, 1 - c))
NEXT_FLIP = permutation(lambda s, z, y, c: (s + 1, z, 1 - y, c))
PREV_FLIP = permutation(lambda s, z, y, c: (s - 1, z, 1 - y, c))
NEXT = permutation(lambda s, z, y, c: (s + 1, z, y, c))
PREV = permutation(lambda s, z, y, c: (s - 1, z, y, c))
Z_GROUPS = [[z * 4 + q for z in range(N_Z)] for q in range(4)]
K_STEPS = 4
N_STEPS = 7


def over_z(values):
    return lax.all_to_all(values, "ep", 0, 0, axis_index_groups=Z_GROUPS, tiled=True)


def dot(a, b):
    return jnp.dot(a, b, preferred_element_type=jnp.float32)


def dot_t(a, b):
    return lax.dot_general(a, b, (((1,), (1,)), ((), ())), preferred_element_type=jnp.float32)


def fill(rows_scr, pieces):
    at = 0
    for piece in pieces:
        rows_scr[pl.ds(at, piece.shape[0]), :] = piece[...]
        at += piece.shape[0]


def emit_columns(tile, outs):
    part, width = outs[0].shape
    step = width // N_STEPS
    for n in range(N_STEPS):
        cols = pl.ds(n * step, step)
        value = tile(cols)
        for i, out in enumerate(outs):
            out[:, cols] = value[i * part:(i + 1) * part].astype(out.dtype)


def over_width(rows_scr, mat, product):
    step = rows_scr.shape[1] // K_STEPS
    total = None
    for k in range(K_STEPS):
        part = pl.ds(k * step, step)
        add = product(rows_scr[:, part], mat(part))
        total = add if total is None else total + add
    return total


def forward_kernel(p0, p1, p2, p3, gate_ref, up_ref, down_ref, k0, k1, s0, s1, slope_ref, gated_ref, x_scr):
    fill(x_scr, (p0, p1, p2, p3))
    gate_val = over_width(x_scr, lambda part: gate_ref[part, :], dot)
    up_val = over_width(x_scr, lambda part: up_ref[part, :], dot)
    sig_val = jax.nn.sigmoid(gate_val)
    gated = gate_val * sig_val
    gated_ref[...] = gated
    slope_ref[...] = up_val * sig_val * (1.0 + gate_val * (1.0 - sig_val))
    hidden = (gated * up_val).astype(jnp.bfloat16)
    emit_columns(lambda cols: dot(hidden, down_ref[:, cols]), (k0, k1, s0, s1))


def backward_kernel(p0, p1, p2, p3, gate_ref, up_ref, down_ref, slope_ref, gated_ref, k0, k1, s0, s1, g_scr):
    fill(g_scr, (p0, p1, p2, p3))
    d_hidden = over_width(g_scr, lambda part: down_ref[:, part], dot_t)
    d_gate = (d_hidden * slope_ref[...]).astype(jnp.bfloat16)
    d_up = (d_hidden * gated_ref[...]).astype(jnp.bfloat16)
    emit_columns(lambda cols: dot_t(d_gate, gate_ref[cols, :]) + dot_t(d_up, up_ref[cols, :]), (k0, k1, s0, s1))


VMEM = pl.BlockSpec(memory_space=pltpu.VMEM)


def expert_call(kernel, pieces, gate_mat, up_mat, down_mat, saved, cost):
    width, hid = gate_mat.shape
    rows = sum(p.shape[0] for p in pieces)
    part = rows // 4
    out_shape = [jax.ShapeDtypeStruct((part, width), t) for t in (jnp.float32, jnp.float32, jnp.bfloat16, jnp.bfloat16)]
    if not saved:
        out_shape += [jax.ShapeDtypeStruct((rows, hid), jnp.float32)] * 2
    operands = (*pieces, *(m for m in (gate_mat, up_mat, down_mat)), *saved)
    return pl.pallas_call(
        kernel,
        out_shape=out_shape,
        in_specs=[VMEM] * len(operands),
        out_specs=[VMEM] * len(out_shape),
        scratch_shapes=[pltpu.VMEM((rows, width), jnp.bfloat16)],
        compiler_params=pltpu.CompilerParams(vmem_limit_bytes=20 * 2**20),
        cost_estimate=pl.CostEstimate(flops=cost, bytes_accessed=12_000_000, transcendentals=0),
    )(*operands)


def mix_kernel(combine_ref, value_ref, out_ref):
    combine = combine_ref[...]
    hi = combine.astype(jnp.bfloat16)
    rest = combine - hi.astype(jnp.float32)
    mid = rest.astype(jnp.bfloat16)
    low = (rest - mid.astype(jnp.float32)).astype(jnp.bfloat16)
    weights = jnp.concatenate([hi, mid, low], axis=1)
    step = out_ref.shape[1] // N_STEPS
    for n in range(N_STEPS):
        cols = pl.ds(n * step, step)
        value = value_ref[:, cols]
        out_ref[:, cols] = dot(weights, jnp.concatenate([value, value, value], axis=0)).astype(jnp.bfloat16)


def mix(combine, values, cost):
    return pl.pallas_call(
        mix_kernel,
        out_shape=jax.ShapeDtypeStruct((combine.shape[0], values.shape[1]), jnp.bfloat16),
        in_specs=[VMEM, VMEM],
        out_specs=VMEM,
        compiler_params=pltpu.CompilerParams(vmem_limit_bytes=20 * 2**20),
        cost_estimate=pl.CostEstimate(flops=cost, bytes_accessed=2_000_000, transcendentals=0),
    )(combine, values)


def shards(acts, cotan, routes, scores, w_gate, w_up, w_down):
    tok_rows, width = acts.shape
    gate_mat, up_mat, down_mat = w_gate[0], w_up[0], w_down[0]
    norm_w = scores / jnp.sum(scores, axis=1, keepdims=True) * ROUTE_SCALE
    match = routes[:, :, None] == jnp.arange(N_Z, dtype=jnp.int32)
    member = jnp.sum(match.astype(jnp.int32), axis=1)
    weight_te = jnp.sum(jnp.where(match, norm_w[:, :, None], 0.0), axis=1)
    slot_of = jnp.cumsum(member, axis=0) - member
    placed = (member[:, :, None] == 1) & (slot_of[:, :, None] == jnp.arange(SLOTS, dtype=jnp.int32))
    dispatch = placed.reshape(tok_rows, ROWS).T.astype(jnp.bfloat16)
    combine = (placed.astype(jnp.float32) * weight_te[:, :, None]).reshape(tok_rows, ROWS)

    together = lax.optimization_barrier

    def to(values, table):
        return lax.ppermute(values, AXES, table)

    def back(values):
        return over_z(values.reshape(N_Z, SLOTS, width)).reshape(ROWS, width)

    def finish(*terms):
        return sum(t.astype(jnp.float32) for t in terms).astype(jnp.bfloat16)

    empty = jnp.zeros_like(placed)
    first = jnp.concatenate([placed, empty], axis=2).reshape(tok_rows, 2 * ROWS).T.astype(jnp.bfloat16)
    second = jnp.concatenate([empty, placed], axis=2).reshape(tok_rows, 2 * ROWS).T.astype(jnp.bfloat16)
    pair = (dot(first, acts) + dot(second, cotan)).astype(jnp.bfloat16)
    pair = over_z(pair.reshape(N_Z, 2 * SLOTS, width))
    x_own, g_own = pair[:, :SLOTS].reshape(ROWS, width), pair[:, SLOTS:].reshape(ROWS, width)
    combine_next = to(combine, NEXT)
    combine_prev = to(combine, PREV)
    x_own, g_own, combine_next, combine_prev = together((x_own, g_own, combine_next, combine_prev))
    x_y = to(x_own, TO_Y)
    x_c = to(x_own, TO_CORE)
    g_c = to(g_own, TO_CORE)
    x_y, x_c, g_c, x_own, g_own = together((x_y, x_c, g_c, x_own, g_own))
    x_cy = to(x_y, TO_CORE)
    keep_a, keep_b, send_a, send_b, slope, gated = expert_call(
        forward_kernel, (x_own, x_y, x_c, x_cy), gate_mat, up_mat, down_mat, (), 20_000_000_000
    )
    g_y = to(g_own, TO_Y)
    send_a, send_b, slope, gated, g_y = together((send_a, send_b, slope, gated, g_y))
    got_a, out_b = to(send_a, TO_CORE), to(send_b, TO_CORE)
    g_cy = to(g_y, TO_CORE)
    out_a = finish(keep_a, got_a)
    out_a, g_cy = together((out_a, g_cy))
    out_y = to(out_a, TO_Y)
    grad_keep_a, grad_keep_b, send_a, send_b = expert_call(
        backward_kernel, (g_own, g_y, g_c, g_cy), gate_mat, up_mat, down_mat, (slope, gated), 20_000_000_000
    )
    got_a, grad_b = to(send_a, TO_CORE), to(send_b, TO_CORE)
    grad_y = to(finish(grad_keep_a, got_a), TO_Y)
    out_rows = back(finish(keep_b, out_b, out_y))
    grad_rows = to(finish(grad_keep_b, grad_b, grad_y), PREV_FLIP)
    out_rows, grad_rows = together((out_rows, grad_rows))
    out_rows = to(out_rows, NEXT_FLIP)
    grad_rows = back(grad_rows)
    return mix(combine_next, out_rows, 500_000_000), mix(combine_prev, grad_rows, 500_000_000)


def solution(mesh):
    rows = P(AXES, None)
    in_specs = (rows, rows, rows, rows, P("pipe", None, "ep"), P("pipe", None, "ep"), P("pipe", "ep", None))
    return jax.shard_map(shards, mesh=mesh, in_specs=in_specs, out_specs=(rows, rows), check_vma=False)
```

```python
import jax
import jax.numpy as jnp
from jax import lax
from jax.experimental import pallas as pl
from jax.experimental.pallas import tpu as pltpu
from jax.sharding import PartitionSpec as P

ROUTE_SCALE = 2.5
N_X, N_YH, N_Z, N_Y, N_C = 4, 2, 8, 2, 2
N_EP = N_Z * N_Y * N_C
AXES = ("pipe", "ep")
SLOTS = 8
ROWS = N_Z * SLOTS


def permutation(target):
    pairs = []
    for s in range(N_X * N_YH):
        for i in range(N_EP):
            z, y, c = i // 4, (i // 2) % 2, i % 2
            s2, z2, y2, c2 = target(s, z, y, c)
            pairs.append((s * N_EP + i, (s2 % 8) * N_EP + (z2 % N_Z) * 4 + y2 * 2 + c2))
    return pairs


TO_Y = permutation(lambda s, z, y, c: (s, z, 1 - y, c))
TO_CORE = permutation(lambda s, z, y, c: (s, z, y, 1 - c))
NEXT_FLIP = permutation(lambda s, z, y, c: (s + 1, z, 1 - y, c))
PREV_FLIP = permutation(lambda s, z, y, c: (s - 1, z, 1 - y, c))
NEXT = permutation(lambda s, z, y, c: (s + 1, z, y, c))
PREV = permutation(lambda s, z, y, c: (s - 1, z, y, c))
Z_GROUPS = [[z * 4 + q for z in range(N_Z)] for q in range(4)]
K_STEPS = 4
N_STEPS = 7


def over_z(values):
    return lax.all_to_all(values, "ep", 0, 0, axis_index_groups=Z_GROUPS, tiled=True)


def dot(a, b):
    return jnp.dot(a, b, preferred_element_type=jnp.float32)


def dot_t(a, b):
    return lax.dot_general(a, b, (((1,), (1,)), ((), ())), preferred_element_type=jnp.float32)


def fill(rows_scr, pieces):
    at = 0
    for piece in pieces:
        rows_scr[pl.ds(at, piece.shape[0]), :] = piece[...]
        at += piece.shape[0]


def emit_columns(tile, outs):
    part, width = outs[0].shape
    step = width // N_STEPS
    for n in range(N_STEPS):
        cols = pl.ds(n * step, step)
        value = tile(cols)
        for i, out in enumerate(outs):
            out[:, cols] = value[i * part:(i + 1) * part].astype(out.dtype)


def over_width(rows_scr, mat, product):
    step = rows_scr.shape[1] // K_STEPS
    total = None
    for k in range(K_STEPS):
        part = pl.ds(k * step, step)
        add = product(rows_scr[:, part], mat(part))
        total = add if total is None else total + add
    return total


def forward_kernel(p0, p1, p2, p3, gate_ref, up_ref, down_ref, k0, k1, s0, s1, slope_ref, gated_ref, x_scr):
    fill(x_scr, (p0, p1, p2, p3))
    gate_val = over_width(x_scr, lambda part: gate_ref[part, :], dot)
    up_val = over_width(x_scr, lambda part: up_ref[part, :], dot)
    sig_val = jax.nn.sigmoid(gate_val)
    gated = gate_val * sig_val
    gated_ref[...] = gated
    slope_ref[...] = up_val * sig_val * (1.0 + gate_val * (1.0 - sig_val))
    hidden = (gated * up_val).astype(jnp.bfloat16)
    emit_columns(lambda cols: dot(hidden, down_ref[:, cols]), (k0, k1, s0, s1))


def backward_kernel(p0, p1, p2, p3, gate_ref, up_ref, down_ref, slope_ref, gated_ref, k0, k1, s0, s1, g_scr):
    fill(g_scr, (p0, p1, p2, p3))
    d_hidden = over_width(g_scr, lambda part: down_ref[:, part], dot_t)
    d_gate = (d_hidden * slope_ref[...]).astype(jnp.bfloat16)
    d_up = (d_hidden * gated_ref[...]).astype(jnp.bfloat16)
    emit_columns(lambda cols: dot_t(d_gate, gate_ref[cols, :]) + dot_t(d_up, up_ref[cols, :]), (k0, k1, s0, s1))


VMEM = pl.BlockSpec(memory_space=pltpu.VMEM)


def expert_call(kernel, pieces, gate_mat, up_mat, down_mat, saved, cost):
    width, hid = gate_mat.shape
    rows = sum(p.shape[0] for p in pieces)
    part = rows // 4
    out_shape = [jax.ShapeDtypeStruct((part, width), jnp.bfloat16)] * 4
    if not saved:
        out_shape += [jax.ShapeDtypeStruct((rows, hid), jnp.float32)] * 2
    operands = (*pieces, *(m for m in (gate_mat, up_mat, down_mat)), *saved)
    return pl.pallas_call(
        kernel,
        out_shape=out_shape,
        in_specs=[VMEM] * len(operands),
        out_specs=[VMEM] * len(out_shape),
        scratch_shapes=[pltpu.VMEM((rows, width), jnp.bfloat16)],
        compiler_params=pltpu.CompilerParams(vmem_limit_bytes=20 * 2**20),
        cost_estimate=pl.CostEstimate(flops=cost, bytes_accessed=12_000_000, transcendentals=0),
    )(*operands)


def mix_kernel(combine_ref, value_ref, out_ref):
    combine = combine_ref[...]
    hi = combine.astype(jnp.bfloat16)
    rest = combine - hi.astype(jnp.float32)
    mid = rest.astype(jnp.bfloat16)
    low = (rest - mid.astype(jnp.float32)).astype(jnp.bfloat16)
    weights = jnp.concatenate([hi, mid, low], axis=1)
    step = out_ref.shape[1] // N_STEPS
    for n in range(N_STEPS):
        cols = pl.ds(n * step, step)
        value = value_ref[:, cols]
        out_ref[:, cols] = dot(weights, jnp.concatenate([value, value, value], axis=0)).astype(jnp.bfloat16)


def mix(combine, values, cost):
    return pl.pallas_call(
        mix_kernel,
        out_shape=jax.ShapeDtypeStruct((combine.shape[0], values.shape[1]), jnp.bfloat16),
        in_specs=[VMEM, VMEM],
        out_specs=VMEM,
        compiler_params=pltpu.CompilerParams(vmem_limit_bytes=20 * 2**20),
        cost_estimate=pl.CostEstimate(flops=cost, bytes_accessed=2_000_000, transcendentals=0),
    )(combine, values)


def shards(acts, cotan, routes, scores, w_gate, w_up, w_down):
    tok_rows, width = acts.shape
    gate_mat, up_mat, down_mat = w_gate[0], w_up[0], w_down[0]
    norm_w = scores / jnp.sum(scores, axis=1, keepdims=True) * ROUTE_SCALE
    match = routes[:, :, None] == jnp.arange(N_Z, dtype=jnp.int32)
    member = jnp.sum(match.astype(jnp.int32), axis=1)
    weight_te = jnp.sum(jnp.where(match, norm_w[:, :, None], 0.0), axis=1)
    slot_of = jnp.cumsum(member, axis=0) - member
    placed = (member[:, :, None] == 1) & (slot_of[:, :, None] == jnp.arange(SLOTS, dtype=jnp.int32))
    dispatch = placed.reshape(tok_rows, ROWS).T.astype(jnp.bfloat16)
    combine = (placed.astype(jnp.float32) * weight_te[:, :, None]).reshape(tok_rows, ROWS)

    together = lax.optimization_barrier

    def to(values, table):
        return lax.ppermute(values, AXES, table)

    def back(values):
        return over_z(values.reshape(N_Z, SLOTS, width)).reshape(ROWS, width)

    def finish(*terms):
        return sum(t.astype(jnp.float32) for t in terms).astype(jnp.bfloat16)

    empty = jnp.zeros_like(placed)
    first = jnp.concatenate([placed, empty], axis=2).reshape(tok_rows, 2 * ROWS).T.astype(jnp.bfloat16)
    second = jnp.concatenate([empty, placed], axis=2).reshape(tok_rows, 2 * ROWS).T.astype(jnp.bfloat16)
    pair = (dot(first, acts) + dot(second, cotan)).astype(jnp.bfloat16)
    pair = over_z(pair.reshape(N_Z, 2 * SLOTS, width))
    x_own, g_own = pair[:, :SLOTS].reshape(ROWS, width), pair[:, SLOTS:].reshape(ROWS, width)
    combine_next = to(combine, NEXT)
    combine_prev = to(combine, PREV)
    x_own, g_own, combine_next, combine_prev = together((x_own, g_own, combine_next, combine_prev))
    x_y = to(x_own, TO_Y)
    x_c = to(x_own, TO_CORE)
    g_c = to(g_own, TO_CORE)
    x_y, x_c, g_c, x_own, g_own = together((x_y, x_c, g_c, x_own, g_own))
    x_cy = to(x_y, TO_CORE)
    keep_a, keep_b, send_a, send_b, slope, gated = expert_call(
        forward_kernel, (x_own, x_y, x_c, x_cy), gate_mat, up_mat, down_mat, (), 20_000_000_000
    )
    g_y = to(g_own, TO_Y)
    slope, gated, g_y = together((slope, gated, g_y))
    got_a, out_b = to(send_a, TO_CORE), to(send_b, TO_CORE)
    g_cy = to(g_y, TO_CORE)
    out_a = finish(keep_a, got_a)
    out_a, g_cy = together((out_a, g_cy))
    out_y = to(out_a, TO_Y)
    grad_keep_a, grad_keep_b, send_a, send_b = expert_call(
        backward_kernel, (g_own, g_y, g_c, g_cy), gate_mat, up_mat, down_mat, (slope, gated), 20_000_000_000
    )
    got_a, grad_b = to(send_a, TO_CORE), to(send_b, TO_CORE)
    grad_y = to(finish(grad_keep_a, got_a), TO_Y)
    out_rows = back(finish(keep_b, out_b, out_y))
    grad_rows = to(finish(grad_keep_b, grad_b, grad_y), PREV_FLIP)
    out_rows, grad_rows = together((out_rows, grad_rows))
    out_rows = to(out_rows, NEXT_FLIP)
    grad_rows = back(grad_rows)
    return mix(combine_next, out_rows, 500_000_000), mix(combine_prev, grad_rows, 500_000_000)


def solution(mesh):
    rows = P(AXES, None)
    in_specs = (rows, rows, rows, rows, P("pipe", None, "ep"), P("pipe", None, "ep"), P("pipe", "ep", None))
    return jax.shard_map(shards, mesh=mesh, in_specs=in_specs, out_specs=(rows, rows), check_vma=False)
```

```python
import jax
import jax.numpy as jnp
from jax import lax
from jax.experimental import pallas as pl
from jax.experimental.pallas import tpu as pltpu
from jax.sharding import PartitionSpec as P

ROUTE_SCALE = 2.5
N_X, N_YH, N_Z, N_Y, N_C = 4, 2, 8, 2, 2
N_EP = N_Z * N_Y * N_C
AXES = ("pipe", "ep")
SLOTS = 8
ROWS = N_Z * SLOTS


def permutation(target):
    pairs = []
    for s in range(N_X * N_YH):
        for i in range(N_EP):
            z, y, c = i // 4, (i // 2) % 2, i % 2
            s2, z2, y2, c2 = target(s, z, y, c)
            pairs.append((s * N_EP + i, (s2 % 8) * N_EP + (z2 % N_Z) * 4 + y2 * 2 + c2))
    return pairs


TO_Y = permutation(lambda s, z, y, c: (s, z, 1 - y, c))
TO_CORE = permutation(lambda s, z, y, c: (s, z, y, 1 - c))
NEXT_FLIP = permutation(lambda s, z, y, c: (s + 1, z, 1 - y, c))
PREV_FLIP = permutation(lambda s, z, y, c: (s - 1, z, 1 - y, c))
NEXT = permutation(lambda s, z, y, c: (s + 1, z, y, c))
PREV = permutation(lambda s, z, y, c: (s - 1, z, y, c))
Z_GROUPS = [[z * 4 + q for z in range(N_Z)] for q in range(4)]
K_STEPS = 4
N_STEPS = 7


def over_z(values):
    return lax.all_to_all(values, "ep", 0, 0, axis_index_groups=Z_GROUPS, tiled=True)


def dot(a, b):
    return jnp.dot(a, b, preferred_element_type=jnp.float32)


def dot_t(a, b):
    return lax.dot_general(a, b, (((1,), (1,)), ((), ())), preferred_element_type=jnp.float32)


def fill(rows_scr, pieces):
    at = 0
    for piece in pieces:
        rows_scr[pl.ds(at, piece.shape[0]), :] = piece[...]
        at += piece.shape[0]


def emit_columns(tile, outs):
    part, width = outs[0].shape
    step = width // N_STEPS
    for n in range(N_STEPS):
        cols = pl.ds(n * step, step)
        value = tile(cols)
        for i, out in enumerate(outs):
            out[:, cols] = value[i * part:(i + 1) * part].astype(out.dtype)


def over_width(rows_scr, mat, product):
    step = rows_scr.shape[1] // K_STEPS
    total = None
    for k in range(K_STEPS):
        part = pl.ds(k * step, step)
        add = product(rows_scr[:, part], mat(part))
        total = add if total is None else total + add
    return total


def forward_kernel(p0, p1, p2, p3, gate_ref, up_ref, down_ref, k0, k1, s0, s1, slope_ref, gated_ref, x_scr):
    fill(x_scr, (p0, p1, p2, p3))
    gate_val = over_width(x_scr, lambda part: gate_ref[part, :], dot)
    up_val = over_width(x_scr, lambda part: up_ref[part, :], dot)
    sig_val = jax.nn.sigmoid(gate_val)
    gated = gate_val * sig_val
    gated_ref[...] = gated
    slope_ref[...] = up_val * sig_val * (1.0 + gate_val * (1.0 - sig_val))
    hidden = (gated * up_val).astype(jnp.bfloat16)
    emit_columns(lambda cols: dot(hidden, down_ref[:, cols]), (k0, k1, s0, s1))


def backward_kernel(p0, p1, p2, p3, gate_ref, up_ref, down_ref, slope_ref, gated_ref, k0, k1, s0, s1, g_scr):
    fill(g_scr, (p0, p1, p2, p3))
    d_hidden = over_width(g_scr, lambda part: down_ref[:, part], dot_t)
    d_gate = (d_hidden * slope_ref[...]).astype(jnp.bfloat16)
    d_up = (d_hidden * gated_ref[...]).astype(jnp.bfloat16)
    emit_columns(lambda cols: dot_t(d_gate, gate_ref[cols, :]) + dot_t(d_up, up_ref[cols, :]), (k0, k1, s0, s1))


VMEM = pl.BlockSpec(memory_space=pltpu.VMEM)


def expert_call(kernel, pieces, gate_mat, up_mat, down_mat, saved, cost):
    width, hid = gate_mat.shape
    rows = sum(p.shape[0] for p in pieces)
    part = rows // 4
    out_shape = [jax.ShapeDtypeStruct((part, width), jnp.bfloat16)] * 4
    if not saved:
        out_shape += [jax.ShapeDtypeStruct((rows, hid), jnp.float32)] * 2
    operands = (*pieces, *(m for m in (gate_mat, up_mat, down_mat)), *saved)
    return pl.pallas_call(
        kernel,
        out_shape=out_shape,
        in_specs=[VMEM] * len(operands),
        out_specs=[VMEM] * len(out_shape),
        scratch_shapes=[pltpu.VMEM((rows, width), jnp.bfloat16)],
        compiler_params=pltpu.CompilerParams(vmem_limit_bytes=20 * 2**20),
        cost_estimate=pl.CostEstimate(flops=cost, bytes_accessed=12_000_000, transcendentals=0),
    )(*operands)


def mix_kernel(combine_ref, value_ref, out_ref, out_scr, sems):
    combine = combine_ref[...]
    hi = combine.astype(jnp.bfloat16)
    rest = combine - hi.astype(jnp.float32)
    mid = rest.astype(jnp.bfloat16)
    low = (rest - mid.astype(jnp.float32)).astype(jnp.bfloat16)
    weights = jnp.concatenate([hi, mid, low], axis=1)
    copies = []
    step = out_ref.shape[1] // N_STEPS
    for n in range(N_STEPS):
        cols = pl.ds(n * step, step)
        value = value_ref[:, cols]
        out_scr[:, cols] = dot(weights, jnp.concatenate([value, value, value], axis=0)).astype(jnp.bfloat16)
        copies.append(pltpu.make_async_copy(out_scr.at[:, cols], out_ref.at[:, cols], sems.at[n]))
        copies[-1].start()
    for copy in copies:
        copy.wait()


def mix(combine, values, cost):
    return pl.pallas_call(
        mix_kernel,
        out_shape=jax.ShapeDtypeStruct((combine.shape[0], values.shape[1]), jnp.bfloat16),
        in_specs=[VMEM, VMEM],
        out_specs=pl.BlockSpec(memory_space=pl.ANY),
        scratch_shapes=[
            pltpu.VMEM((combine.shape[0], values.shape[1]), jnp.bfloat16),
            pltpu.SemaphoreType.DMA((N_STEPS,)),
        ],
        compiler_params=pltpu.CompilerParams(vmem_limit_bytes=20 * 2**20),
        cost_estimate=pl.CostEstimate(flops=cost, bytes_accessed=2_000_000, transcendentals=0),
    )(combine, values)


def shards(acts, cotan, routes, scores, w_gate, w_up, w_down):
    tok_rows, width = acts.shape
    gate_mat, up_mat, down_mat = w_gate[0], w_up[0], w_down[0]
    norm_w = scores / jnp.sum(scores, axis=1, keepdims=True) * ROUTE_SCALE
    match = routes[:, :, None] == jnp.arange(N_Z, dtype=jnp.int32)
    member = jnp.sum(match.astype(jnp.int32), axis=1)
    weight_te = jnp.sum(jnp.where(match, norm_w[:, :, None], 0.0), axis=1)
    slot_of = jnp.cumsum(member, axis=0) - member
    placed = (member[:, :, None] == 1) & (slot_of[:, :, None] == jnp.arange(SLOTS, dtype=jnp.int32))
    dispatch = placed.reshape(tok_rows, ROWS).T.astype(jnp.bfloat16)
    combine = (placed.astype(jnp.float32) * weight_te[:, :, None]).reshape(tok_rows, ROWS)

    together = lax.optimization_barrier

    def to(values, table):
        return lax.ppermute(values, AXES, table)

    def back(values):
        return over_z(values.reshape(N_Z, SLOTS, width)).reshape(ROWS, width)

    def finish(*terms):
        return sum(t.astype(jnp.float32) for t in terms).astype(jnp.bfloat16)

    empty = jnp.zeros_like(placed)
    first = jnp.concatenate([placed, empty], axis=2).reshape(tok_rows, 2 * ROWS).T.astype(jnp.bfloat16)
    second = jnp.concatenate([empty, placed], axis=2).reshape(tok_rows, 2 * ROWS).T.astype(jnp.bfloat16)
    pair = (dot(first, acts) + dot(second, cotan)).astype(jnp.bfloat16)
    pair = over_z(pair.reshape(N_Z, 2 * SLOTS, width))
    x_own, g_own = pair[:, :SLOTS].reshape(ROWS, width), pair[:, SLOTS:].reshape(ROWS, width)
    combine_next = to(combine, NEXT)
    combine_prev = to(combine, PREV)
    x_own, g_own, combine_next, combine_prev = together((x_own, g_own, combine_next, combine_prev))
    x_y = to(x_own, TO_Y)
    x_c = to(x_own, TO_CORE)
    g_c = to(g_own, TO_CORE)
    x_y, x_c, g_c, x_own, g_own = together((x_y, x_c, g_c, x_own, g_own))
    x_cy = to(x_y, TO_CORE)
    keep_a, keep_b, send_a, send_b, slope, gated = expert_call(
        forward_kernel, (x_own, x_y, x_c, x_cy), gate_mat, up_mat, down_mat, (), 20_000_000_000
    )
    g_y = to(g_own, TO_Y)
    slope, gated, g_y = together((slope, gated, g_y))
    got_a, out_b = to(send_a, TO_CORE), to(send_b, TO_CORE)
    g_cy = to(g_y, TO_CORE)
    out_a = finish(keep_a, got_a)
    out_a, g_cy = together((out_a, g_cy))
    out_y = to(out_a, TO_Y)
    grad_keep_a, grad_keep_b, send_a, send_b = expert_call(
        backward_kernel, (g_own, g_y, g_c, g_cy), gate_mat, up_mat, down_mat, (slope, gated), 20_000_000_000
    )
    got_a, grad_b = to(send_a, TO_CORE), to(send_b, TO_CORE)
    grad_y = to(finish(grad_keep_a, got_a), TO_Y)
    out_rows = back(finish(keep_b, out_b, out_y))
    grad_rows = to(finish(grad_keep_b, grad_b, grad_y), PREV_FLIP)
    out_rows, grad_rows = together((out_rows, grad_rows))
    out_rows = to(out_rows, NEXT_FLIP)
    grad_rows = back(grad_rows)
    return mix(combine_next, out_rows, 500_000_000), mix(combine_prev, grad_rows, 500_000_000)


def solution(mesh):
    rows = P(AXES, None)
    in_specs = (rows, rows, rows, rows, P("pipe", None, "ep"), P("pipe", None, "ep"), P("pipe", "ep", None))
    return jax.shard_map(shards, mesh=mesh, in_specs=in_specs, out_specs=(rows, rows), check_vma=False)
```
